512 devices in a mesh: segment: 4 (over y), seq: 16 (over z), head: 8 (over x, core).
Axes of the slice: x: 4, y: 4, z: 16, core: 2. Of those that a mesh axis runs over, the one named last changes fastest.
Arguments:
- queries: bfloat16 [8192, 8192], P(('segment', 'seq', 'head')), may hold values from -38 to 38
- span_keys: bfloat16 [8192, 1024], P(('segment', 'seq', 'head')), may hold values from -4 to 4
- span_values: bfloat16 [8192, 1024], P(('segment', 'seq', 'head')), may hold values from -4 to 4
- cache_keys: bfloat16 [128, 128, 8, 128], P('seq', None, 'head'), may hold values from -4 to 4
- cache_values: bfloat16 [128, 128, 8, 128], P('seq', None, 'head'), may hold values from -4 to 4
- hit_holder: int32 [128], replicated, may hold values from 0 to 15, as said below
- hit_slot: int32 [128], replicated, may hold values from 0 to 7
- sparse_lists: int32 [64, 8, 8], replicated, may hold values from 0 to 127, as said below
Outputs:
- attended: bfloat16 [8192, 8192], P(('segment', 'seq'), 'head')
The draws below stay inside these ranges and needn't reach their ends.
Inputs may be any that keep to these rules, and one draw needn't show every extreme that they name: hit_holder and hit_slot together name every pair of holder and slot exactly once, so each holder keeps 8 prefix blocks. `sparse_lists`: A list names 8 different blocks; they are kept by exactly 8 different holders, 1 block from each.
All inputs are finite; a program needn't handle non-finite values.
Results may differ from the reference program's by a relative error of at most 0.0049.
Values may be sent and summed in bfloat16 or wider, within the bound.
A program may use at most 64 MiB of HBM per device.

```python
import jax
import jax.numpy as jnp
from jax import lax

QH = 64
KVH = 8
HD = 128
BLK = 128
SEL = 8
CAP = 1
HOLD_BLK = 8
QPG = 8
SPAN = 8192
NQB = 64
NPB = 128


def span_key_base(key):
    base_key = jax.random.fold_in(key, 101)
    keys_drawn = jnp.clip(jax.random.normal(base_key, (SPAN, KVH * HD), jnp.float32), -4.0, 4.0)
    return keys_drawn


def draw_span_keys(key, part):
    return span_key_base(key).astype(jnp.bfloat16)


def draw_queries(key, part):
    query_key = jax.random.fold_in(key, 202)
    drawn = jnp.clip(jax.random.normal(query_key, (SPAN, QH * HD), jnp.float32), -4.0, 4.0)
    drawn = 3.0 * drawn
    return drawn.astype(jnp.bfloat16)


def prefix_perm(key):
    return jax.random.permutation(jax.random.fold_in(key, 303), NPB).astype(jnp.int32)


def draw_hit_holder(key, part):
    return (prefix_perm(key) // HOLD_BLK).astype(jnp.int32)


def draw_hit_slot(key, part):
    return (prefix_perm(key) % HOLD_BLK).astype(jnp.int32)


def draw_sparse_lists(key, part):
    holder_total = NPB // HOLD_BLK
    perm_drawn = prefix_perm(key)
    inverse = jnp.argsort(perm_drawn).astype(jnp.int32)
    list_total = NQB * KVH
    group_total = SEL // CAP
    holder_scores = jax.random.randint(jax.random.fold_in(key, 404), (list_total, holder_total), 0, 1 << 20) * holder_total + jnp.arange(holder_total)
    holders_used = jnp.argsort(holder_scores, axis=1)[:, :group_total]
    slot_scores = jax.random.randint(jax.random.fold_in(key, 405), (list_total, group_total, HOLD_BLK), 0, 1 << 20) * HOLD_BLK + jnp.arange(HOLD_BLK)
    slots_used = jnp.argsort(slot_scores, axis=2)[:, :, :CAP]
    positions = holders_used[:, :, None] * HOLD_BLK + slots_used
    blocks_named = jnp.take(inverse, positions.reshape(list_total, SEL), axis=0)
    order_scores = jax.random.randint(jax.random.fold_in(key, 406), (list_total, SEL), 0, 1 << 20) * SEL + jnp.arange(SEL)
    shuffled = jnp.take_along_axis(blocks_named, jnp.argsort(order_scores, axis=1), axis=1)
    return shuffled.reshape(NQB, KVH, SEL).astype(jnp.int32)


def block_levels(stream_key, extent, split, least, largest):
    def one(axis_at, blocks):
        heights = jax.random.uniform(jax.random.fold_in(jax.random.fold_in(stream_key, 6), axis_at), (blocks,), jnp.float32, least / len(split), largest / len(split))
        return jnp.repeat(jnp.exp(heights), extent[axis_at] // blocks).reshape((-1,) + (1,) * (len(extent) - axis_at - 1))

    gain = one(*split[0])
    for cut in split[1:]:
        gain = gain * one(*cut)
    return gain


def normal_values(stream_key, shape, width, bound, shards=(), held_as=jnp.bfloat16):
    result = width * jax.random.normal(stream_key, shape, jnp.float32)
    if shards:
        result = result * block_levels(stream_key, shape, shards, -0.22, 0.18)
    return jnp.clip(result, -bound, bound).astype(held_as)


def setup_inputs(seed: int = 0) -> dict:
    key_list = jax.random.split(jax.random.key(seed), 9)
    return {
        "queries": draw_queries(jax.random.fold_in(key_list[8], 71), 0),
        "span_keys": draw_span_keys(jax.random.fold_in(key_list[8], 71), 0),
        "span_values": normal_values(key_list[2], (SPAN, KVH * HD), 1.0, 4.0, ((0, 512),)),
        "cache_keys": normal_values(key_list[3], (NPB, BLK, KVH, HD), 1.0, 4.0, ((0, 16), (2, 8))),
        "cache_values": normal_values(key_list[4], (NPB, BLK, KVH, HD), 1.0, 4.0, ((0, 16), (2, 8))),
        "hit_holder": draw_hit_holder(jax.random.fold_in(key_list[8], 71), 0),
        "hit_slot": draw_hit_slot(jax.random.fold_in(key_list[8], 71), 0),
        "sparse_lists": draw_sparse_lists(jax.random.fold_in(key_list[8], 71), 0),
    }


def reference(queries, span_keys, span_values, cache_keys, cache_values, hit_holder, hit_slot, sparse_lists):
    score_scale = HD ** -0.5
    cache_rows = (hit_holder * HOLD_BLK + hit_slot).astype(jnp.int32)
    zero_index = jnp.zeros((), jnp.int32)

    def one_block(flat_index):
        flat_index = flat_index.astype(jnp.int32)
        block_idx = (flat_index // KVH).astype(jnp.int32)
        kv_group = (flat_index % KVH).astype(jnp.int32)
        query_rows = lax.dynamic_slice(queries, ((block_idx * BLK).astype(jnp.int32), (kv_group * QPG * HD).astype(jnp.int32)), (BLK, QPG * HD))
        query_rows = query_rows.astype(jnp.float32).reshape(BLK * QPG, HD)
        head_col = (kv_group * HD).astype(jnp.int32)
        span_k = lax.dynamic_slice(span_keys, (zero_index, head_col), (SPAN, HD)).astype(jnp.float32)
        span_v = lax.dynamic_slice(span_values, (zero_index, head_col), (SPAN, HD)).astype(jnp.float32)
        chosen = lax.dynamic_slice(sparse_lists, (block_idx, kv_group, zero_index), (1, 1, SEL)).reshape(SEL)
        rows_used = jnp.take(cache_rows, chosen.astype(jnp.int32), axis=0)
        head_keys = lax.dynamic_index_in_dim(cache_keys, kv_group, 2, keepdims=False)
        head_values = lax.dynamic_index_in_dim(cache_values, kv_group, 2, keepdims=False)
        prefix_k = jnp.take(head_keys, rows_used, axis=0).reshape(SEL * BLK, HD).astype(jnp.float32)
        prefix_v = jnp.take(head_values, rows_used, axis=0).reshape(SEL * BLK, HD).astype(jnp.float32)
        prefix_scores = jnp.dot(query_rows, prefix_k.T, precision=lax.Precision.HIGHEST) * score_scale
        span_scores = jnp.dot(query_rows, span_k.T, precision=lax.Precision.HIGHEST) * score_scale
        query_pos = block_idx * BLK + jnp.arange(BLK * QPG, dtype=jnp.int32) // QPG
        causal = jnp.arange(SPAN, dtype=jnp.int32)[None, :] <= query_pos[:, None]
        span_scores = jnp.where(causal, span_scores, -jnp.inf)
        scores = jnp.concatenate([prefix_scores, span_scores], axis=1)
        row_peak = jnp.max(scores, axis=1, keepdims=True)
        weights = jnp.exp(scores - row_peak)
        row_total = jnp.sum(weights, axis=1, keepdims=True)
        rounded = lax.optimization_barrier(weights.astype(jnp.bfloat16)).astype(jnp.float32)
        values_all = jnp.concatenate([prefix_v, span_v], axis=0)
        mixed = jnp.dot(rounded, values_all, precision=lax.Precision.HIGHEST) / row_total
        return mixed.astype(jnp.bfloat16).reshape(BLK, QPG * HD)

    stacked = lax.map(one_block, jnp.arange(NQB * KVH, dtype=jnp.int32))
    stacked = stacked.reshape(NQB, KVH, BLK, QPG * HD).transpose(0, 2, 1, 3)
    return stacked.reshape(SPAN, QH * HD)
```

```python
import functools

import jax
import jax.numpy as jnp
from jax import lax
from jax.experimental import pallas as pl
from jax.experimental.pallas import tpu as pltpu
from jax.sharding import PartitionSpec as P

HD = 128
BLK = 128
SEL = 8
HOLD_BLK = 8
QPG = 8
LOG2E = 1.4426950408889634
SCALE = HD ** -0.5 * LOG2E
NT = (((1,), (1,)), ((), ()))
NN = (((1,), (0,)), ((), ()))


def wait_bytes(ref, sem):
    pltpu.make_async_copy(ref, ref, sem).wait()


def kernel(
    ny, nz, nh,
    q_in, k_in, v_in, ck, cv, hold, slot, lists, out,
    qb, sk, sv, pk, pv, bias, acc, peak, sendo, recvo, sendl, recvl, kp, vp, lists_s,
    q_send, q_recv, kv_send, kv_recv, ring_send, ring_recv, o_send, o_recv, l_send, l_recv,
    own_sem, list_sem,
):
    y, z, h = lax.axis_index("segment"), lax.axis_index("seq"), lax.axis_index("head")
    plane = ny * nh
    me = y * nh + h
    rows = BLK // nh
    stripe = BLK // ny
    per = nh // ny
    right, left = lax.rem(z + 1, nz), lax.rem(z + nz - 1, nz)
    half = nz // 2

    own_rows = pl.ds(pl.multiple_of(y * stripe, stripe), stripe)
    own_slots = pl.ds(z * HOLD_BLK, HOLD_BLK)
    own_k = pltpu.make_async_copy(ck.at[:, own_rows, :], pk.at[own_slots], own_sem.at[0])
    own_v = pltpu.make_async_copy(cv.at[:, own_rows, :], pv.at[own_slots], own_sem.at[1])
    get_lists = pltpu.make_async_copy(lists.at[h], lists_s, list_sem)

    barrier = pltpu.get_barrier_semaphore()

    def greet(o, _):
        i = lax.rem(me + o, plane)
        pl.semaphore_signal(
            barrier, inc=1, device_id={"segment": lax.div(i, nh), "head": lax.rem(i, nh)}
        )
        return 0

    pl.semaphore_signal(barrier, inc=1, device_id={"seq": left})
    pl.semaphore_signal(barrier, inc=1, device_id={"seq": right})
    lax.fori_loop(1, plane, greet, 0)
    own_k.start()
    own_v.start()
    get_lists.start()
    pl.semaphore_wait(barrier, plane + 1)

    tables = (sk, sv, pk, pv)

    def piece(kind, origin):
        if kind < 2:
            return tables[kind].at[:, origin]
        return tables[kind].at[pl.ds(origin * HOLD_BLK, HOLD_BLK)]

    def steps(kind, way):
        return half if kind % 2 == way else half - 1

    def ring_copy(kind, way, step, src, origin):
        return pltpu.make_async_remote_copy(
            src_ref=src,
            dst_ref=piece(kind, origin),
            send_sem=ring_send.at[kind * 2 + way, step],
            recv_sem=ring_recv.at[kind * 2 + way, step],
            device_id={"seq": left if way else right},
        )

    def origin_at(way, step):
        return lax.rem(z + step, nz) if way else lax.rem(z + nz - step, nz)

    def relay(kind, way, step):
        origin = origin_at(way, step)
        last = steps(kind, way)

        def go():
            wait_bytes(piece(kind, origin), ring_recv.at[kind * 2 + way, step - 1])

        def send():
            ring_copy(kind, way, step, piece(kind, origin), origin).start()

        if isinstance(step, int):
            if step <= last:
                go()
            if step < last:
                send()
        else:
            pl.when(step <= last)(go)
            pl.when(step < last)(send)

    for way in (0, 1):
        for kind, src in ((2, ck), (3, cv)):
            if steps(kind, way) > 0:
                ring_copy(kind, way, 0, src.at[:, own_rows, :], z).start()

    target = lax.div(h, per)
    dst_rows = pl.ds(pl.multiple_of(lax.rem(h, per) * rows, rows), rows)

    def head_cols(i, width):
        return pl.ds(pl.multiple_of(i * width, width), width)

    def send_kv(o, _):
        i = lax.rem(h + o, nh)
        here = (target == y) & (i == h)

        def local_copy():
            for n, (src, tab) in enumerate(((k_in, sk), (v_in, sv))):
                pltpu.make_async_copy(
                    src.at[:, head_cols(i, HD)], tab.at[y, z, dst_rows], kv_recv.at[n]
                ).start()

        def remote_copy():
            for n, (src, tab) in enumerate(((k_in, sk), (v_in, sv))):
                pltpu.make_async_remote_copy(
                    src_ref=src.at[:, head_cols(i, HD)],
                    dst_ref=tab.at[y, z, dst_rows],
                    send_sem=kv_send.at[n],
                    recv_sem=kv_recv.at[n],
                    device_id={"segment": target, "head": i},
                ).start()

        pl.when(here)(local_copy)
        pl.when(jnp.logical_not(here))(remote_copy)
        return 0

    lax.fori_loop(0, nh, send_kv, 0)

    pltpu.make_async_copy(q_in.at[:, head_cols(h, QPG * HD)], qb.at[me], q_recv).start()

    def send_q(o, _):
        i = lax.rem(me + o, plane)
        g = lax.rem(i, nh)
        pltpu.make_async_remote_copy(
            src_ref=q_in.at[:, head_cols(g, QPG * HD)],
            dst_ref=qb.at[me],
            send_sem=q_send,
            recv_sem=q_recv,
            device_id={"segment": lax.div(i, nh), "head": g},
        ).start()
        return 0

    lax.fori_loop(1, plane, send_q, 0)

    width = nz * stripe
    row_id = lax.broadcasted_iota(jnp.int32, (BLK, width), 0)
    col_id = lax.broadcasted_iota(jnp.int32, (BLK, width), 1)
    key_pos = lax.div(col_id, stripe) * BLK + lax.rem(col_id, stripe) + y * stripe
    bias[...] = jnp.where(key_pos <= z * BLK + row_id, 0.0, -1e30).astype(jnp.float32)

    for n, tab in enumerate((sk, sv)):
        wait_bytes(tab.at[:, z], kv_recv.at[n])
        for way in (0, 1):
            if steps(n, way) > 0:
                ring_copy(n, way, 0, piece(n, z), z).start()

    def span_step(s, _):
        for kind in (0, 1):
            for way in (0, 1):
                relay(kind, way, s)
        return 0

    lax.fori_loop(1, half + 1, span_step, 0)
    wait_bytes(qb, q_recv)

    def query_pair(yp, pair):
        parts = [
            qb[pl.ds(yp * nh, nh), :, head_cols(pair * 2 + j, HD)].reshape(BLK, HD)
            for j in (0, 1)
        ]
        return jnp.concatenate(parts, axis=0)

    def span_unit(yp, pair):
        n = (yp + 1) * width
        keys = sk[0 : yp + 1].reshape(n, HD)
        values = sv[0 : yp + 1].reshape(n, HD)
        values = jnp.concatenate([values, jnp.ones_like(values)], axis=1)
        s = lax.dot_general(query_pair(yp, pair), keys, NT, preferred_element_type=jnp.float32)
        b = bias[...]
        last = s[:, n - width :] + jnp.concatenate([b, b], axis=0)
        s = jnp.concatenate([s[:, : n - width], last], axis=1) if yp else last
        m = jnp.max(s, axis=1, keepdims=True) * SCALE
        w = jnp.exp2(s * SCALE - m).astype(jnp.bfloat16)
        r = lax.dot_general(w, values, NN, preferred_element_type=jnp.float32)
        m = jnp.broadcast_to(m, (2 * BLK, HD))
        for j in (0, 1):
            acc[yp * QPG + pair * 2 + j] = r[j * BLK : (j + 1) * BLK]
            peak[yp * QPG + pair * 2 + j] = m[j * BLK : (j + 1) * BLK]

    def span_pair(pair, _):
        for part in (0, 1):
            s = 2 * pair + 1 + part
            for kind in (2, 3):
                for way in (0, 1):
                    relay(kind, way, s)
            for yp in range(ny - 1, -1, -1):
                if (yp == ny - 1) == (part == 0):
                    span_unit(yp, pair)
        return 0

    lax.fori_loop(0, QPG // 2, span_pair, 0)

    own_k.wait()
    own_v.wait()
    get_lists.wait()
    lane = lax.broadcasted_iota(jnp.int32, (BLK, HD), 1)

    order = sorted(range(ny), key=lambda o: (o == 0, -min(o, ny - o)))
    for o in order:
        yp = lax.rem(y + o, ny)
        for i in range(SEL):
            block = lists_s[i, yp * nz + z]
            at = hold[block] * HOLD_BLK + slot[block]
            kp[i * stripe : (i + 1) * stripe, :] = pk[at]
            vp[i * stripe : (i + 1) * stripe, :] = pv[at]

        def prefix_pair(pair, level):
            values = vp[...]
            values = jnp.concatenate([values, jnp.ones_like(values)], axis=1)
            s = lax.dot_general(
                query_pair(yp, pair), kp[...], NT, preferred_element_type=jnp.float32
            )
            base = yp * QPG + pair * 2
            m1 = jnp.concatenate([peak[base], peak[base + 1]], axis=0)
            m = jnp.maximum(m1, jnp.max(s, axis=1, keepdims=True) * SCALE)
            mm = jnp.concatenate([m] * (SEL * stripe // HD), axis=1)
            w = jnp.exp2(s * SCALE - mm).astype(jnp.bfloat16)
            r = lax.dot_general(w, values, NN, preferred_element_type=jnp.float32)
            fade = jnp.exp2(m1 - m)
            a = jnp.concatenate([acc[base], acc[base + 1]], axis=0)
            total = a[:, HD:] * fade + r[:, HD:]
            mixed = ((a[:, :HD] * fade + r[:, :HD]) / total).astype(jnp.bfloat16)
            lse = m + jnp.log2(total)
            for j in (0, 1):
                sendo[yp, :, head_cols(pair * 2 + j, HD)] = mixed[j * BLK : (j + 1) * BLK]
                level = jnp.where(lane == pair * 2 + j, lse[j * BLK : (j + 1) * BLK], level)
            if o:
                cols = head_cols(pair, 2 * HD)
                pltpu.make_async_remote_copy(
                    src_ref=sendo.at[yp, :, cols],
                    dst_ref=recvo.at[y, :, cols],
                    send_sem=o_send.at[o],
                    recv_sem=o_recv.at[o],
                    device_id={"segment": yp},
                ).start()
            return level

        level = lax.fori_loop(0, QPG // 2, prefix_pair, jnp.zeros((BLK, HD), jnp.float32))
        sendl[yp] = level.T[:QPG]
        if o:
            pltpu.make_async_remote_copy(
                src_ref=sendl.at[yp],
                dst_ref=recvl.at[y],
                send_sem=l_send.at[o],
                recv_sem=l_recv.at[o],
                device_id={"segment": yp},
            ).start()

    levels = [sendl[y]]
    parts = [sendo.at[y]]
    for o in order[:-1]:
        src = lax.rem(y + ny - o, ny)
        wait_bytes(recvl.at[src], l_recv.at[o])
        wait_bytes(recvo.at[src], o_recv.at[o])
        levels.append(recvl[src])
        parts.append(recvo.at[src])
    top = functools.reduce(jnp.maximum, levels)
    shares = [jnp.exp2(v - top) for v in levels]
    norm = 1.0 / functools.reduce(jnp.add, shares)
    fill = jnp.zeros((BLK - QPG, BLK), jnp.float32)
    shares = [jnp.concatenate([v * norm, fill], axis=0).T for v in shares]
    for p in range(QPG):
        cols = slice(p * HD, (p + 1) * HD)
        out[:, cols] = functools.reduce(
            jnp.add,
            [w[:, p : p + 1] * part[:, cols].astype(jnp.float32) for w, part in zip(shares, parts)],
        ).astype(jnp.bfloat16)

    wait_bytes(qb.at[: plane - 1], q_send)
    for n, src in enumerate((k_in, v_in)):
        pl.when(target == y)(
            functools.partial(wait_bytes, src.at[:, : (nh - 1) * HD], kv_send.at[n])
        )
        pl.when(target != y)(functools.partial(wait_bytes, src, kv_send.at[n]))
    for kind in range(4):
        for way in (0, 1):
            count = steps(kind, way)

            def sent(step, _, kind=kind, way=way):
                wait_bytes(piece(kind, z), ring_send.at[kind * 2 + way, step])
                return 0

            lax.fori_loop(0, count, sent, 0)
    for o in range(1, ny):
        wait_bytes(sendo.at[0], o_send.at[o])
        wait_bytes(sendl.at[0], l_send.at[o])


def local(ny, nz, nh, q, k, v, ck, cv, hold, slot, lists):
    rows, width, stripe = BLK // nh, QPG * HD, BLK // ny
    blocks = ck.shape[0] * nz
    ck = ck.reshape(ck.shape[0], BLK, HD)
    cv = cv.reshape(cv.shape[0], BLK, HD)
    lists = jnp.transpose(lists, (1, 2, 0))
    any_, smem = pl.BlockSpec(memory_space=pl.ANY), pl.BlockSpec(memory_space=pltpu.SMEM)
    bf, f32, dma = jnp.bfloat16, jnp.float32, pltpu.SemaphoreType.DMA
    return pl.pallas_call(
        functools.partial(kernel, ny, nz, nh),
        out_shape=jax.ShapeDtypeStruct((BLK, width), bf),
        in_specs=[any_] * 5 + [smem, smem, any_],
        out_specs=pl.BlockSpec(memory_space=pltpu.VMEM),
        scratch_shapes=[
            pltpu.VMEM((ny * nh, rows, width), bf),
            pltpu.VMEM((ny, nz, stripe, HD), bf),
            pltpu.VMEM((ny, nz, stripe, HD), bf),
            pltpu.VMEM((blocks, stripe, HD), bf),
            pltpu.VMEM((blocks, stripe, HD), bf),
            pltpu.VMEM((BLK, nz * stripe), f32),
            pltpu.VMEM((ny * QPG, BLK, 2 * HD), f32),
            pltpu.VMEM((ny * QPG, BLK, HD), f32),
            pltpu.VMEM((ny, BLK, width), bf),
            pltpu.VMEM((ny, BLK, width), bf),
            pltpu.VMEM((ny, QPG, BLK), f32),
            pltpu.VMEM((ny, QPG, BLK), f32),
            pltpu.VMEM((SEL * stripe, HD), bf),
            pltpu.VMEM((SEL * stripe, HD), bf),
            pltpu.SMEM((SEL, lists.shape[2]), jnp.int32),
            dma, dma, dma((2,)), dma((2,)),
            dma((8, nz // 2)), dma((8, nz // 2)),
            dma((ny,)), dma((ny,)), dma((ny,)), dma((ny,)),
            dma((2,)), dma,
        ],
        compiler_params=pltpu.CompilerParams(
            collective_id=0, has_side_effects=True, vmem_limit_bytes=52 * 2**20
        ),
        cost_estimate=pl.CostEstimate(
            flops=4 * BLK * QPG * HD * 6144, bytes_accessed=2**24, transcendentals=6144 * 1024
        ),
        name="attend",
    )(q, k, v, ck, cv, hold, slot, lists)


def solution(mesh):
    ny, nz, nh = mesh.shape["segment"], mesh.shape["seq"], mesh.shape["head"]
    placed = (
        P(("segment", "seq", "head"), None),
        P(("segment", "seq", "head"), None),
        P(("segment", "seq", "head"), None),
        P("seq", None, "head", None),
        P("seq", None, "head", None),
        P(),
        P(),
        P(),
    )
    return jax.shard_map(
        functools.partial(local, ny, nz, nh),
        mesh=mesh,
        in_specs=placed,
        out_specs=P(("segment", "seq"), "head"),
        check_vma=False,
    )
```

```python
import functools

import jax
import jax.numpy as jnp
from jax import lax
from jax.experimental import pallas as pl
from jax.experimental.pallas import tpu as pltpu
from jax.sharding import PartitionSpec as P

HD = 128
BLK = 128
SEL = 8
HOLD_BLK = 8
QPG = 8
GROUP = 4
LOG2E = 1.4426950408889634
SCALE = HD ** -0.5 * LOG2E
NT = (((1,), (1,)), ((), ()))
NN = (((1,), (0,)), ((), ()))


def wait_bytes(ref, sem):
    pltpu.make_async_copy(ref, ref, sem).wait()


def kernel(
    ny, nz, nh,
    q_in, k_in, v_in, ck, cv, hold, slot, lists, out,
    qb, sk, sv, pk, pv, kc, vc, bias, acc, peak, sendo, recvo, sendl, recvl, kp, vp, lists_s,
    q_send, q_recv, kv_send, kv_recv, ring_send, ring_recv, o_send, o_recv,
    own_sem, list_sem,
):
    y, z, h = lax.axis_index("segment"), lax.axis_index("seq"), lax.axis_index("head")
    plane = ny * nh
    me = y * nh + h
    rows = BLK // nh
    stripe = BLK // ny
    per = nh // ny
    right, left = lax.rem(z + 1, nz), lax.rem(z + nz - 1, nz)
    half = nz // 2

    own_rows = pl.ds(pl.multiple_of(y * stripe, stripe), stripe)
    own_slots = pl.ds(z * HOLD_BLK, HOLD_BLK)
    own_k = pltpu.make_async_copy(ck.at[:, own_rows, :], pk.at[own_slots], own_sem.at[0])
    own_v = pltpu.make_async_copy(cv.at[:, own_rows, :], pv.at[own_slots], own_sem.at[1])
    get_lists = pltpu.make_async_copy(lists.at[h], lists_s, list_sem)

    barrier = pltpu.get_barrier_semaphore()

    ys = [lax.rem(y + d, ny) for d in range(ny)]
    hs = [lax.rem(h + d, nh) for d in range(nh)]
    peers = [(dy, dh) for dy in range(ny) for dh in range(nh) if dy or dh]
    peers.sort(key=lambda p: -min(p[0], ny - p[0]) - min(p[1], nh - p[1]) // 2)
    for dy, dh in peers:
        pl.semaphore_signal(barrier, inc=1, device_id={"segment": ys[dy], "head": hs[dh]})
    for side in (left, right):
        pl.semaphore_signal(barrier, inc=1, device_id={"seq": side})
    own_k.start()
    own_v.start()
    get_lists.start()
    pl.semaphore_wait(barrier, plane + 1)

    tables = (sk, sv, pk, pv)

    def piece(kind, origin):
        if kind < 2:
            return tables[kind].at[:, origin]
        return tables[kind].at[pl.ds(origin * HOLD_BLK, HOLD_BLK)]

    def steps(kind, way):
        return half if kind % 2 == way else half - 1

    def ring_copy(kind, way, step, src, origin):
        return pltpu.make_async_remote_copy(
            src_ref=src,
            dst_ref=piece(kind, origin),
            send_sem=ring_send.at[kind * 2 + way, step],
            recv_sem=ring_recv.at[kind * 2 + way, step],
            device_id={"seq": left if way else right},
        )

    def origin_at(way, step):
        return lax.rem(z + step, nz) if way else lax.rem(z + nz - step, nz)

    def relay(kind, way, step):
        origin = origin_at(way, step)
        last = steps(kind, way)

        def go():
            wait_bytes(piece(kind, origin), ring_recv.at[kind * 2 + way, step - 1])

        def send():
            ring_copy(kind, way, step, piece(kind, origin), origin).start()

        if isinstance(step, int):
            if step <= last:
                go()
            if step < last:
                send()
        else:
            pl.when(step <= last)(go)
            pl.when(step < last)(send)

    for way in (0, 1):
        for kind, src in ((2, ck), (3, cv)):
            if steps(kind, way) > 0:
                ring_copy(kind, way, 0, src.at[:, own_rows, :], z).start()

    target = lax.div(h, per)
    dst_rows = pl.ds(pl.multiple_of(lax.rem(h, per) * rows, rows), rows)

    def head_cols(i, width):
        return pl.ds(pl.multiple_of(i * width, width), width)

    def send_kv(dh, local_copy):
        for n, (src, tab) in enumerate(((k_in, sk), (v_in, sv))):
            src, dst = src.at[:, head_cols(hs[dh], HD)], tab.at[y, z, dst_rows]
            if local_copy:
                pltpu.make_async_copy(src, dst, kv_recv.at[n]).start()
            else:
                pltpu.make_async_remote_copy(
                    src_ref=src,
                    dst_ref=dst,
                    send_sem=kv_send.at[n],
                    recv_sem=kv_recv.at[n],
                    device_id={"segment": target, "head": hs[dh]},
                ).start()

    for dh in sorted(range(nh), key=lambda d: -min(d, nh - d)):
        if dh:
            send_kv(dh, False)
        else:
            pl.when(target == y)(lambda: send_kv(0, True))
            pl.when(target != y)(lambda: send_kv(0, False))

    def send_queries():
        pltpu.make_async_copy(q_in.at[:, head_cols(h, QPG * HD)], qb.at[me], q_recv).start()
        for dy, dh in peers:
            pltpu.make_async_remote_copy(
                src_ref=q_in.at[:, head_cols(hs[dh], QPG * HD)],
                dst_ref=qb.at[me],
                send_sem=q_send,
                recv_sem=q_recv,
                device_id={"segment": ys[dy], "head": hs[dh]},
            ).start()

    acc[...] = jnp.zeros_like(acc)
    peak[...] = jnp.full(peak.shape, -1e30, jnp.float32)

    def ring_step(s, kinds):
        for kind in kinds:
            for way in (0, 1):
                relay(kind, way, s)

    for n, tab in enumerate((sk, sv)):
        wait_bytes(tab.at[:, z], kv_recv.at[n])
        for way in (0, 1):
            if steps(n, way) > 0:
                ring_copy(n, way, 0, piece(n, z), z).start()
    ring_step(1, (2, 3))
    send_queries()
    ring_step(1, (0, 1))

    def queries_of(yp, group):
        parts = [
            qb[pl.ds(yp * nh, nh), :, head_cols(group * GROUP + j, HD)].reshape(BLK, HD)
            for j in range(GROUP)
        ]
        return jnp.concatenate(parts, axis=0)

    def fold(yp, group, keys, values, mask, keep):
        s = lax.dot_general(queries_of(yp, group), keys, NT, preferred_element_type=jnp.float32)
        if mask is not None:
            n = s.shape[1] - mask.shape[1]
            tail = s[:, n:] + jnp.concatenate([mask] * GROUP, axis=0)
            s = jnp.concatenate([s[:, :n], tail], axis=1) if n else tail
        values = jnp.concatenate([values, jnp.ones_like(values)], axis=1)
        heads = pl.ds(yp * QPG + group * GROUP, GROUP)
        m1 = peak[heads].reshape(GROUP * BLK, HD)
        m = jnp.maximum(m1, jnp.max(s, axis=1, keepdims=True) * SCALE)
        mm = jnp.concatenate([m] * (s.shape[1] // HD), axis=1)
        w = jnp.exp2(s * SCALE - mm).astype(jnp.bfloat16)
        r = lax.dot_general(w, values, NN, preferred_element_type=jnp.float32)
        fade = jnp.exp2(m1 - m)
        fade = jnp.concatenate([fade, fade], axis=1)
        a = acc[heads].reshape(GROUP * BLK, 2 * HD) * fade + r
        if keep:
            acc[heads] = a.reshape(GROUP, BLK, 2 * HD)
            peak[heads] = m.reshape(GROUP, BLK, HD)
        return m, a

    def take_chunk(chunk):
        places = [
            lax.rem(z + 2 * chunk, nz),
            lax.rem(z + nz - 2 * chunk - 1, nz),
            lax.rem(z + 2 * chunk + 1, nz),
            lax.rem(z + nz - 2 * chunk - 2, nz),
        ]
        row = lax.broadcasted_iota(jnp.int32, (BLK, 4 * stripe), 0)
        col = lax.broadcasted_iota(jnp.int32, (BLK, 4 * stripe), 1)
        key_pos = lax.rem(col, stripe) + y * stripe
        for i, place in enumerate(places):
            key_pos = key_pos + jnp.where(lax.div(col, stripe) == i, place * BLK, 0)
            for yp in range(ny):
                rows_i = slice(i * stripe, (i + 1) * stripe)
                kc[yp, rows_i, :] = sk[yp, place]
                vc[yp, rows_i, :] = sv[yp, place]
        bias[...] = jnp.where(key_pos <= z * BLK + row, 0.0, -1e30).astype(jnp.float32)

    def span_half(t):
        pl.when(lax.rem(t, 2) == 0)(lambda: take_chunk(lax.div(t, 2)))
        for yp in range(ny):
            n = (yp + 1) * 4 * stripe
            keys = kc[0 : yp + 1].reshape(n, HD)
            values = vc[0 : yp + 1].reshape(n, HD)
            fold(yp, lax.rem(t, 2), keys, values, bias[...], True)

    chunks = half // 2 - 1
    first = half - chunks

    def step_body(s, _):
        ring_step(s, (2, 3))
        pl.when(s == first)(functools.partial(wait_bytes, qb, q_recv))
        at = 2 * (s - first)
        pl.when(s >= first)(lambda: span_half(at))
        ring_step(s, (0, 1))
        pl.when(s >= first)(lambda: span_half(at + 1))
        return 0

    lax.fori_loop(2, half, step_body, 0)
    ring_step(half, (2, 3))
    if chunks == 0:
        wait_bytes(qb, q_recv)
    own_k.wait()
    own_v.wait()
    get_lists.wait()

    def prefix(yp):
        for i in range(SEL):
            block = lists_s[i, yp * nz + z]
            at = hold[block] * HOLD_BLK + slot[block]
            kp[i * stripe : (i + 1) * stripe, :] = pk[at]
            vp[i * stripe : (i + 1) * stripe, :] = pv[at]
        for group in range(QPG // GROUP):
            fold(yp, group, kp[...], vp[...], None, True)

    lane = lax.broadcasted_iota(jnp.int32, (BLK, HD), 1)
    order = sorted(range(ny), key=lambda o: (o == 0, -min(o, ny - o)))
    for o in order:
        yp = ys[o]
        prefix(yp)
        if o == order[0]:
            ring_step(half, (0, 1))
            take_chunk(half // 2 - 1)
        keys = kc[...].reshape(ny * 4 * stripe, HD)
        values = vc[...].reshape(ny * 4 * stripe, HD)
        mask = jnp.concatenate(
            [
                jnp.where(jnp.full(bias.shape, i, jnp.int32) < yp, 0.0, bias[...])
                + jnp.where(jnp.full(bias.shape, i, jnp.int32) > yp, -1e30, 0.0)
                for i in range(ny)
            ],
            axis=1,
        )
        for group in range(QPG // GROUP):
            m, a = fold(yp, group, keys, values, mask, False)
            total = a[:, HD:]
            mixed = (a[:, :HD] / total).astype(jnp.bfloat16)
            lse = m + jnp.log2(total)
            level = jnp.zeros((BLK, HD), jnp.float32)
            for j in range(GROUP):
                rows_j = slice(j * BLK, (j + 1) * BLK)
                cols = slice((group * GROUP + j) * HD, (group * GROUP + j + 1) * HD)
                sendo[yp, :, cols] = mixed[rows_j]
                level = jnp.where(lane == j, lse[rows_j], level)
            sendl[yp, group] = level.T[:8]
            if o:
                cols = slice(group * GROUP * HD, (group + 1) * GROUP * HD)
                for n, (src, dst) in enumerate(
                    (
                        (sendl.at[yp, group], recvl.at[y, group]),
                        (sendo.at[yp, :, cols], recvo.at[y, :, cols]),
                    )
                ):
                    pltpu.make_async_remote_copy(
                        src_ref=src,
                        dst_ref=dst,
                        send_sem=o_send.at[n, o, group],
                        recv_sem=o_recv.at[n, o, group],
                        device_id={"segment": yp},
                    ).start()

    fill = jnp.zeros((BLK - 8, BLK), jnp.float32)
    for group in range(QPG // GROUP):
        cols = slice(group * GROUP * HD, (group + 1) * GROUP * HD)
        levels = [sendl[y, group]]
        parts = [sendo.at[y]]
        for o in order[:-1]:
            src = lax.rem(y + ny - o, ny)
            wait_bytes(recvl.at[src, group], o_recv.at[0, o, group])
            wait_bytes(recvo.at[src, :, cols], o_recv.at[1, o, group])
            levels.append(recvl[src, group])
            parts.append(recvo.at[src])
        top = functools.reduce(jnp.maximum, levels)
        shares = [jnp.exp2(v - top) for v in levels]
        norm = 1.0 / functools.reduce(jnp.add, shares)
        shares = [jnp.concatenate([v * norm, fill], axis=0).T for v in shares]
        for j in range(GROUP):
            cols = slice((group * GROUP + j) * HD, (group * GROUP + j + 1) * HD)
            out[:, cols] = functools.reduce(
                jnp.add,
                [
                    w[:, j : j + 1] * part[:, cols].astype(jnp.float32)
                    for w, part in zip(shares, parts)
                ],
            ).astype(jnp.bfloat16)

    wait_bytes(qb.at[: plane - 1], q_send)
    for n, src in enumerate((k_in, v_in)):
        pl.when(target == y)(
            functools.partial(wait_bytes, src.at[:, : (nh - 1) * HD], kv_send.at[n])
        )
        pl.when(target != y)(functools.partial(wait_bytes, src, kv_send.at[n]))
    for kind in range(4):
        for way in (0, 1):
            count = steps(kind, way)

            def sent(step, _, kind=kind, way=way):
                wait_bytes(piece(kind, z), ring_send.at[kind * 2 + way, step])
                return 0

            lax.fori_loop(0, count, sent, 0)
    for o in range(1, ny):
        for group in range(QPG // GROUP):
            wait_bytes(sendl.at[0, group], o_send.at[0, o, group])
            wait_bytes(sendo.at[0, :, : GROUP * HD], o_send.at[1, o, group])


def local(ny, nz, nh, q, k, v, ck, cv, hold, slot, lists):
    rows, width, stripe = BLK // nh, QPG * HD, BLK // ny
    blocks = ck.shape[0] * nz
    ck = ck.reshape(ck.shape[0], BLK, HD)
    cv = cv.reshape(cv.shape[0], BLK, HD)
    lists = jnp.transpose(lists, (1, 2, 0))
    hbm, smem = pl.BlockSpec(memory_space=pltpu.HBM), pl.BlockSpec(memory_space=pltpu.SMEM)
    bf, f32, dma = jnp.bfloat16, jnp.float32, pltpu.SemaphoreType.DMA
    return pl.pallas_call(
        functools.partial(kernel, ny, nz, nh),
        out_shape=jax.ShapeDtypeStruct((BLK, width), bf),
        in_specs=[hbm] * 5 + [smem, smem, hbm],
        out_specs=pl.BlockSpec(memory_space=pltpu.VMEM),
        scratch_shapes=[
            pltpu.VMEM((ny * nh, rows, width), bf),
            pltpu.VMEM((ny, nz, stripe, HD), bf),
            pltpu.VMEM((ny, nz, stripe, HD), bf),
            pltpu.VMEM((blocks, stripe, HD), bf),
            pltpu.VMEM((blocks, stripe, HD), bf),
            pltpu.VMEM((ny, 4 * stripe, HD), bf),
            pltpu.VMEM((ny, 4 * stripe, HD), bf),
            pltpu.VMEM((BLK, 4 * stripe), f32),
            pltpu.VMEM((ny * QPG, BLK, 2 * HD), f32),
            pltpu.VMEM((ny * QPG, BLK, HD), f32),
            pltpu.VMEM((ny, BLK, width), bf),
            pltpu.VMEM((ny, BLK, width), bf),
            pltpu.VMEM((ny, QPG // GROUP, 8, BLK), f32),
            pltpu.VMEM((ny, QPG // GROUP, 8, BLK), f32),
            pltpu.VMEM((SEL * stripe, HD), bf),
            pltpu.VMEM((SEL * stripe, HD), bf),
            pltpu.SMEM((SEL, lists.shape[2]), jnp.int32),
            dma, dma, dma((2,)), dma((2,)),
            dma((8, nz // 2)), dma((8, nz // 2)),
            dma((2, ny, QPG // GROUP)), dma((2, ny, QPG // GROUP)),
            dma((2,)), dma,
        ],
        compiler_params=pltpu.CompilerParams(
            collective_id=0, has_side_effects=True, vmem_limit_bytes=60 * 2**20
        ),
        cost_estimate=pl.CostEstimate(
            flops=4 * BLK * QPG * HD * 6144, bytes_accessed=2**24, transcendentals=6144 * 1024
        ),
        name="attend",
    )(q, k, v, ck, cv, hold, slot, lists)


def solution(mesh):
    ny, nz, nh = mesh.shape["segment"], mesh.shape["seq"], mesh.shape["head"]
    placed = (
        P(("segment", "seq", "head"), None),
        P(("segment", "seq", "head"), None),
        P(("segment", "seq", "head"), None),
        P("seq", None, "head", None),
        P("seq", None, "head", None),
        P(),
        P(),
        P(),
    )
    return jax.shard_map(
        functools.partial(local, ny, nz, nh),
        mesh=mesh,
        in_specs=placed,
        out_specs=P(("segment", "seq"), "head"),
        check_vma=False,
    )
```

```python
import functools

import jax
import jax.numpy as jnp
from jax import lax
from jax.experimental import pallas as pl
from jax.experimental.pallas import tpu as pltpu
from jax.sharding import PartitionSpec as P

HD = 128
BLK = 128
SEL = 8
HOLD_BLK = 8
QPG = 8
GROUP = 4
LOG2E = 1.4426950408889634
SCALE = HD ** -0.5 * LOG2E
NT = (((1,), (1,)), ((), ()))
NN = (((1,), (0,)), ((), ()))


def wait_bytes(ref, sem):
    pltpu.make_async_copy(ref, ref, sem).wait()


def kernel(
    ny, nz, nh,
    q_in, k_in, v_in, ck, cv, hold_in, slot_in, lists, out,
    qb, sk, sv, pk, pv, kc, vc, bias, acc, peak, sendo, recvo, sendl, recvl, kp, vp, lists_s, hold, slot,
    q_send, q_recv, kv_send, kv_recv, ring_send, ring_recv, o_send, o_recv,
    own_sem, list_sem,
):
    y, z, h = lax.axis_index("segment"), lax.axis_index("seq"), lax.axis_index("head")
    plane = ny * nh
    me = y * nh + h
    rows = BLK // nh
    stripe = BLK // ny
    per = nh // ny
    right, left = lax.rem(z + 1, nz), lax.rem(z + nz - 1, nz)
    half = nz // 2

    own_rows = pl.ds(pl.multiple_of(y * stripe, stripe), stripe)
    own_slots = pl.ds(z * HOLD_BLK, HOLD_BLK)
    own_k = pltpu.make_async_copy(ck.at[:, own_rows, :], pk.at[own_slots], own_sem.at[0])
    own_v = pltpu.make_async_copy(cv.at[:, own_rows, :], pv.at[own_slots], own_sem.at[1])
    indices = [
        pltpu.make_async_copy(src, dst, list_sem.at[n])
        for n, (src, dst) in enumerate(((lists.at[h], lists_s), (hold_in, hold), (slot_in, slot)))
    ]

    barrier = pltpu.get_barrier_semaphore()

    ys = [lax.rem(y + d, ny) for d in range(ny)]
    hs = [lax.rem(h + d, nh) for d in range(nh)]
    peers = [(dy, dh) for dy in range(ny) for dh in range(nh) if dy or dh]
    peers.sort(key=lambda p: -min(p[0], ny - p[0]) - min(p[1], nh - p[1]) // 2)
    for dy, dh in peers:
        pl.semaphore_signal(barrier, inc=1, device_id={"segment": ys[dy], "head": hs[dh]})
    for side in (left, right):
        pl.semaphore_signal(barrier, inc=1, device_id={"seq": side})
    own_k.start()
    own_v.start()
    for copy in indices:
        copy.start()
    pl.semaphore_wait(barrier, plane + 1)

    tables = (sk, sv, pk, pv)

    def piece(kind, origin):
        if kind < 2:
            return tables[kind].at[:, origin]
        return tables[kind].at[pl.ds(origin * HOLD_BLK, HOLD_BLK)]

    def steps(kind, way):
        return half if kind % 2 == way else half - 1

    def ring_copy(kind, way, step, src, origin):
        return pltpu.make_async_remote_copy(
            src_ref=src,
            dst_ref=piece(kind, origin),
            send_sem=ring_send.at[kind * 2 + way, step],
            recv_sem=ring_recv.at[kind * 2 + way, step],
            device_id={"seq": left if way else right},
        )

    def origin_at(way, step):
        return lax.rem(z + step, nz) if way else lax.rem(z + nz - step, nz)

    def relay(kind, way, step):
        origin = origin_at(way, step)
        last = steps(kind, way)

        def go():
            wait_bytes(piece(kind, origin), ring_recv.at[kind * 2 + way, step - 1])

        def send():
            ring_copy(kind, way, step, piece(kind, origin), origin).start()

        if isinstance(step, int):
            if step <= last:
                go()
            if step < last:
                send()
        else:
            pl.when(step <= last)(go)
            pl.when(step < last)(send)

    for way in (0, 1):
        for kind, src in ((2, ck), (3, cv)):
            if steps(kind, way) > 0:
                ring_copy(kind, way, 0, src.at[:, own_rows, :], z).start()

    target = lax.div(h, per)
    dst_rows = pl.ds(pl.multiple_of(lax.rem(h, per) * rows, rows), rows)

    def head_cols(i, width):
        return pl.ds(pl.multiple_of(i * width, width), width)

    def send_kv(dh, local_copy):
        for n, (src, tab) in enumerate(((k_in, sk), (v_in, sv))):
            src, dst = src.at[:, head_cols(hs[dh], HD)], tab.at[y, z, dst_rows]
            if local_copy:
                pltpu.make_async_copy(src, dst, kv_recv.at[n]).start()
            else:
                pltpu.make_async_remote_copy(
                    src_ref=src,
                    dst_ref=dst,
                    send_sem=kv_send.at[n],
                    recv_sem=kv_recv.at[n],
                    device_id={"segment": target, "head": hs[dh]},
                ).start()

    for dh in sorted(range(nh), key=lambda d: -min(d, nh - d)):
        if dh:
            send_kv(dh, False)
        else:
            pl.when(target == y)(lambda: send_kv(0, True))
            pl.when(target != y)(lambda: send_kv(0, False))

    def send_queries():
        pltpu.make_async_copy(q_in.at[:, head_cols(h, QPG * HD)], qb.at[me], q_recv).start()
        for dy, dh in peers:
            pltpu.make_async_remote_copy(
                src_ref=q_in.at[:, head_cols(hs[dh], QPG * HD)],
                dst_ref=qb.at[me],
                send_sem=q_send,
                recv_sem=q_recv,
                device_id={"segment": ys[dy], "head": hs[dh]},
            ).start()

    def ring_step(s, kinds):
        for kind in kinds:
            for way in (0, 1):
                relay(kind, way, s)

    for n, tab in enumerate((sk, sv)):
        wait_bytes(tab.at[:, z], kv_recv.at[n])
        for way in (0, 1):
            if steps(n, way) > 0:
                ring_copy(n, way, 0, piece(n, z), z).start()
    ring_step(1, (2, 3))
    send_queries()
    ring_step(1, (0, 1))
    acc[...] = jnp.zeros_like(acc)
    peak[...] = jnp.full(peak.shape, -1e30, jnp.float32)

    def queries_of(yp, group):
        parts = [
            qb[pl.ds(yp * nh, nh), :, head_cols(group * GROUP + j, HD)].reshape(BLK, HD)
            for j in range(GROUP)
        ]
        return jnp.concatenate(parts, axis=0)

    def fold(yp, group, keys, values, mask, keep):
        s = lax.dot_general(queries_of(yp, group), keys, NT, preferred_element_type=jnp.float32)
        if mask is not None:
            n = s.shape[1] - mask.shape[1]
            tail = s[:, n:] + jnp.concatenate([mask] * GROUP, axis=0)
            s = jnp.concatenate([s[:, :n], tail], axis=1) if n else tail
        values = jnp.concatenate([values, jnp.ones_like(values)], axis=1)
        heads = pl.ds(yp * QPG + group * GROUP, GROUP)
        m1 = peak[heads].reshape(GROUP * BLK, HD)
        m = jnp.maximum(m1, jnp.max(s, axis=1, keepdims=True) * SCALE)
        mm = jnp.concatenate([m] * (s.shape[1] // HD), axis=1)
        w = jnp.exp2(s * SCALE - mm).astype(jnp.bfloat16)
        r = lax.dot_general(w, values, NN, preferred_element_type=jnp.float32)
        fade = jnp.exp2(m1 - m)
        fade = jnp.concatenate([fade, fade], axis=1)
        a = acc[heads].reshape(GROUP * BLK, 2 * HD) * fade + r
        if keep:
            acc[heads] = a.reshape(GROUP, BLK, 2 * HD)
            peak[heads] = m.reshape(GROUP, BLK, HD)
        return m, a

    def take_chunk(chunk):
        places = [
            lax.rem(z + 2 * chunk, nz),
            lax.rem(z + nz - 2 * chunk - 1, nz),
            lax.rem(z + 2 * chunk + 1, nz),
            lax.rem(z + nz - 2 * chunk - 2, nz),
        ]
        row = lax.broadcasted_iota(jnp.int32, (BLK, 4 * stripe), 0)
        col = lax.broadcasted_iota(jnp.int32, (BLK, 4 * stripe), 1)
        key_pos = lax.rem(col, stripe) + y * stripe
        for i, place in enumerate(places):
            key_pos = key_pos + jnp.where(lax.div(col, stripe) == i, place * BLK, 0)
            for yp in range(ny):
                rows_i = slice(i * stripe, (i + 1) * stripe)
                kc[yp, rows_i, :] = sk[yp, place]
                vc[yp, rows_i, :] = sv[yp, place]
        bias[...] = jnp.where(key_pos <= z * BLK + row, 0.0, -1e30).astype(jnp.float32)

    def span_half(t):
        pl.when(lax.rem(t, 2) == 0)(lambda: take_chunk(lax.div(t, 2)))
        for yp in range(ny):
            n = (yp + 1) * 4 * stripe
            keys = kc[0 : yp + 1].reshape(n, HD)
            values = vc[0 : yp + 1].reshape(n, HD)
            fold(yp, lax.rem(t, 2), keys, values, bias[...], True)

    chunks = half // 2 - 1
    first = half - chunks

    def step_body(s, _):
        ring_step(s, (2, 0))
        pl.when(s == first)(functools.partial(wait_bytes, qb, q_recv))
        at = 2 * (s - first)
        pl.when(s >= first)(lambda: span_half(at))
        ring_step(s, (3, 1))
        pl.when(s >= first)(lambda: span_half(at + 1))
        return 0

    lax.fori_loop(2, half, step_body, 0)
    ring_step(half, (2, 3))
    if chunks == 0:
        wait_bytes(qb, q_recv)
    own_k.wait()
    own_v.wait()
    for copy in indices:
        copy.wait()

    def prefix(yp):
        for i in range(SEL):
            block = lists_s[i, yp * nz + z]
            at = hold[block] * HOLD_BLK + slot[block]
            kp[i * stripe : (i + 1) * stripe, :] = pk[at]
            vp[i * stripe : (i + 1) * stripe, :] = pv[at]
        for group in range(QPG // GROUP):
            fold(yp, group, kp[...], vp[...], None, True)

    lane = lax.broadcasted_iota(jnp.int32, (BLK, HD), 1)
    order = sorted(range(ny), key=lambda o: (o == 0, -min(o, ny - o)))
    for o in order:
        yp = ys[o]
        prefix(yp)
        if o == order[0]:
            ring_step(half, (0, 1))
            take_chunk(half // 2 - 1)
        keys = kc[...].reshape(ny * 4 * stripe, HD)
        values = vc[...].reshape(ny * 4 * stripe, HD)
        mask = jnp.concatenate(
            [
                jnp.where(jnp.full(bias.shape, i, jnp.int32) < yp, 0.0, bias[...])
                + jnp.where(jnp.full(bias.shape, i, jnp.int32) > yp, -1e30, 0.0)
                for i in range(ny)
            ],
            axis=1,
        )
        for group in range(QPG // GROUP):
            m, a = fold(yp, group, keys, values, mask, False)
            total = a[:, HD:]
            mixed = (a[:, :HD] / total).astype(jnp.bfloat16)
            lse = m + jnp.log2(total)
            level = jnp.zeros((BLK, HD), jnp.float32)
            for j in range(GROUP):
                rows_j = slice(j * BLK, (j + 1) * BLK)
                cols = slice((group * GROUP + j) * HD, (group * GROUP + j + 1) * HD)
                sendo[yp, :, cols] = mixed[rows_j]
                level = jnp.where(lane == j, lse[rows_j], level)
            sendl[yp, group] = level.T[:8]
            if o:
                cols = slice(group * GROUP * HD, (group + 1) * GROUP * HD)
                for n, (src, dst) in enumerate(
                    (
                        (sendl.at[yp, group], recvl.at[y, group]),
                        (sendo.at[yp, :, cols], recvo.at[y, :, cols]),
                    )
                ):
                    pltpu.make_async_remote_copy(
                        src_ref=src,
                        dst_ref=dst,
                        send_sem=o_send.at[n, o, group],
                        recv_sem=o_recv.at[n, o, group],
                        device_id={"segment": yp},
                    ).start()

    fill = jnp.zeros((BLK - 8, BLK), jnp.float32)
    for group in range(QPG // GROUP):
        cols = slice(group * GROUP * HD, (group + 1) * GROUP * HD)
        levels = [sendl[y, group]]
        parts = [sendo.at[y]]
        for o in order[:-1]:
            src = lax.rem(y + ny - o, ny)
            wait_bytes(recvl.at[src, group], o_recv.at[0, o, group])
            wait_bytes(recvo.at[src, :, cols], o_recv.at[1, o, group])
            levels.append(recvl[src, group])
            parts.append(recvo.at[src])
        top = functools.reduce(jnp.maximum, levels)
        shares = [jnp.exp2(v - top) for v in levels]
        norm = 1.0 / functools.reduce(jnp.add, shares)
        shares = [jnp.concatenate([v * norm, fill], axis=0).T for v in shares]
        for j in range(GROUP):
            cols = slice((group * GROUP + j) * HD, (group * GROUP + j + 1) * HD)
            out[:, cols] = functools.reduce(
                jnp.add,
                [
                    w[:, j : j + 1] * part[:, cols].astype(jnp.float32)
                    for w, part in zip(shares, parts)
                ],
            ).astype(jnp.bfloat16)

    wait_bytes(qb.at[: plane - 1], q_send)
    for n, src in enumerate((k_in, v_in)):
        pl.when(target == y)(
            functools.partial(wait_bytes, src.at[:, : (nh - 1) * HD], kv_send.at[n])
        )
        pl.when(target != y)(functools.partial(wait_bytes, src, kv_send.at[n]))
    for kind in range(4):
        for way in (0, 1):
            count = steps(kind, way)

            def sent(step, _, kind=kind, way=way):
                wait_bytes(piece(kind, z), ring_send.at[kind * 2 + way, step])
                return 0

            lax.fori_loop(0, count, sent, 0)
    for o in range(1, ny):
        for group in range(QPG // GROUP):
            wait_bytes(sendl.at[0, group], o_send.at[0, o, group])
            wait_bytes(sendo.at[0, :, : GROUP * HD], o_send.at[1, o, group])


def local(ny, nz, nh, q, k, v, ck, cv, hold, slot, lists):
    rows, width, stripe = BLK // nh, QPG * HD, BLK // ny
    blocks = ck.shape[0] * nz
    ck = ck.reshape(ck.shape[0], BLK, HD)
    cv = cv.reshape(cv.shape[0], BLK, HD)
    lists = jnp.transpose(lists, (1, 2, 0))
    hbm = pl.BlockSpec(memory_space=pltpu.HBM)
    bf, f32, dma = jnp.bfloat16, jnp.float32, pltpu.SemaphoreType.DMA
    return pl.pallas_call(
        functools.partial(kernel, ny, nz, nh),
        out_shape=jax.ShapeDtypeStruct((BLK, width), bf),
        in_specs=[hbm] * 8,
        out_specs=pl.BlockSpec(memory_space=pltpu.VMEM),
        scratch_shapes=[
            pltpu.VMEM((ny * nh, rows, width), bf),
            pltpu.VMEM((ny, nz, stripe, HD), bf),
            pltpu.VMEM((ny, nz, stripe, HD), bf),
            pltpu.VMEM((blocks, stripe, HD), bf),
            pltpu.VMEM((blocks, stripe, HD), bf),
            pltpu.VMEM((ny, 4 * stripe, HD), bf),
            pltpu.VMEM((ny, 4 * stripe, HD), bf),
            pltpu.VMEM((BLK, 4 * stripe), f32),
            pltpu.VMEM((ny * QPG, BLK, 2 * HD), f32),
            pltpu.VMEM((ny * QPG, BLK, HD), f32),
            pltpu.VMEM((ny, BLK, width), bf),
            pltpu.VMEM((ny, BLK, width), bf),
            pltpu.VMEM((ny, QPG // GROUP, 8, BLK), f32),
            pltpu.VMEM((ny, QPG // GROUP, 8, BLK), f32),
            pltpu.VMEM((SEL * stripe, HD), bf),
            pltpu.VMEM((SEL * stripe, HD), bf),
            pltpu.SMEM((SEL, lists.shape[2]), jnp.int32),
            pltpu.SMEM(hold.shape, jnp.int32),
            pltpu.SMEM(slot.shape, jnp.int32),
            dma, dma, dma((2,)), dma((2,)),
            dma((8, nz // 2)), dma((8, nz // 2)),
            dma((2, ny, QPG // GROUP)), dma((2, ny, QPG // GROUP)),
            dma((2,)), dma((3,)),
        ],
        compiler_params=pltpu.CompilerParams(
            collective_id=0, has_side_effects=True, vmem_limit_bytes=60 * 2**20
        ),
        cost_estimate=pl.CostEstimate(
            flops=4 * BLK * QPG * HD * 6144, bytes_accessed=2**24, transcendentals=6144 * 1024
        ),
        name="attend",
    )(q, k, v, ck, cv, hold, slot, lists)


def solution(mesh):
    ny, nz, nh = mesh.shape["segment"], mesh.shape["seq"], mesh.shape["head"]
    placed = (
        P(("segment", "seq", "head"), None),
        P(("segment", "seq", "head"), None),
        P(("segment", "seq", "head"), None),
        P("seq", None, "head", None),
        P("seq", None, "head", None),
        P(),
        P(),
        P(),
    )
    return jax.shard_map(
        functools.partial(local, ny, nz, nh),
        mesh=mesh,
        in_specs=placed,
        out_specs=P(("segment", "seq"), "head"),
        check_vma=False,
    )
```

```python
import functools

import jax
import jax.numpy as jnp
from jax import lax
from jax.experimental import pallas as pl
from jax.experimental.pallas import tpu as pltpu
from jax.sharding import PartitionSpec as P

HD = 128
BLK = 128
SEL = 8
HOLD_BLK = 8
QPG = 8
GROUP = 4
LOG2E = 1.4426950408889634
SCALE = HD ** -0.5 * LOG2E
NT = (((1,), (1,)), ((), ()))
NN = (((1,), (0,)), ((), ()))


def wait_bytes(ref, sem):
    pltpu.make_async_copy(ref, ref, sem).wait()


def kernel(
    ny, nz, nh,
    q_in, k_in, v_in, ck, cv, hold_in, slot_in, lists, out,
    qb, sk, sv, pk, pv, kc, vc, bias, acc, peak, sendo, recvo, sendl, recvl, kp, vp, lists_s, hold, slot,
    q_send, q_recv, kv_send, kv_recv, ring_send, ring_recv, o_send, o_recv,
    own_sem, list_sem,
):
    y, z, h = lax.axis_index("segment"), lax.axis_index("seq"), lax.axis_index("head")
    plane = ny * nh
    me = y * nh + h
    rows = BLK // nh
    stripe = BLK // ny
    per = nh // ny
    right, left = lax.rem(z + 1, nz), lax.rem(z + nz - 1, nz)
    half = nz // 2

    own_rows = pl.ds(pl.multiple_of(y * stripe, stripe), stripe)
    own_slots = pl.ds(z * HOLD_BLK, HOLD_BLK)
    own_k = pltpu.make_async_copy(ck.at[:, own_rows, :], pk.at[own_slots], own_sem.at[0])
    own_v = pltpu.make_async_copy(cv.at[:, own_rows, :], pv.at[own_slots], own_sem.at[1])
    indices = [
        pltpu.make_async_copy(src, dst, list_sem.at[n])
        for n, (src, dst) in enumerate(((lists.at[h], lists_s), (hold_in, hold), (slot_in, slot)))
    ]

    barrier = pltpu.get_barrier_semaphore()

    ys = [lax.rem(y + d, ny) for d in range(ny)]
    hs = [lax.rem(h + d, nh) for d in range(nh)]
    peers = [(dy, dh) for dy in range(ny) for dh in range(nh) if dy or dh]
    peers.sort(key=lambda p: -min(p[0], ny - p[0]) - min(p[1], nh - p[1]) // 2)
    for dy, dh in peers:
        pl.semaphore_signal(barrier, inc=1, device_id={"segment": ys[dy], "head": hs[dh]})
    for side in (left, right):
        pl.semaphore_signal(barrier, inc=1, device_id={"seq": side})
    own_k.start()
    own_v.start()
    for copy in indices:
        copy.start()
    pl.semaphore_wait(barrier, plane + 1)

    tables = (sk, sv, pk, pv)

    def piece(kind, origin):
        if kind < 2:
            return tables[kind].at[:, origin]
        return tables[kind].at[pl.ds(origin * HOLD_BLK, HOLD_BLK)]

    def steps(kind, way):
        return half if kind % 2 == way else half - 1

    def ring_copy(kind, way, step, src, origin):
        return pltpu.make_async_remote_copy(
            src_ref=src,
            dst_ref=piece(kind, origin),
            send_sem=ring_send.at[kind * 2 + way, step],
            recv_sem=ring_recv.at[kind * 2 + way, step],
            device_id={"seq": left if way else right},
        )

    def origin_at(way, step):
        return lax.rem(z + step, nz) if way else lax.rem(z + nz - step, nz)

    def relay(kind, way, step):
        origin = origin_at(way, step)
        last = steps(kind, way)

        def go():
            wait_bytes(piece(kind, origin), ring_recv.at[kind * 2 + way, step - 1])

        def send():
            ring_copy(kind, way, step, piece(kind, origin), origin).start()

        if isinstance(step, int):
            if step <= last:
                go()
            if step < last:
                send()
        else:
            pl.when(step <= last)(go)
            pl.when(step < last)(send)

    for way in (0, 1):
        for kind, src in ((2, ck), (3, cv)):
            if steps(kind, way) > 0:
                ring_copy(kind, way, 0, src.at[:, own_rows, :], z).start()

    target = lax.div(h, per)
    dst_rows = pl.ds(pl.multiple_of(lax.rem(h, per) * rows, rows), rows)

    def head_cols(i, width):
        return pl.ds(pl.multiple_of(i * width, width), width)

    def send_kv(dh, local_copy):
        for n, (src, tab) in enumerate(((k_in, sk), (v_in, sv))):
            src, dst = src.at[:, head_cols(hs[dh], HD)], tab.at[y, z, dst_rows]
            if local_copy:
                pltpu.make_async_copy(src, dst, kv_recv.at[n]).start()
            else:
                pltpu.make_async_remote_copy(
                    src_ref=src,
                    dst_ref=dst,
                    send_sem=kv_send.at[n],
                    recv_sem=kv_recv.at[n],
                    device_id={"segment": target, "head": hs[dh]},
                ).start()

    for dh in sorted(range(nh), key=lambda d: -min(d, nh - d)):
        if dh:
            send_kv(dh, False)
        else:
            pl.when(target == y)(lambda: send_kv(0, True))
            pl.when(target != y)(lambda: send_kv(0, False))

    def send_queries():
        pltpu.make_async_copy(q_in.at[:, head_cols(h, QPG * HD)], qb.at[me], q_recv).start()
        for dy, dh in peers:
            pltpu.make_async_remote_copy(
                src_ref=q_in.at[:, head_cols(hs[dh], QPG * HD)],
                dst_ref=qb.at[me],
                send_sem=q_send,
                recv_sem=q_recv,
                device_id={"segment": ys[dy], "head": hs[dh]},
            ).start()

    def ring_step(s, kinds):
        for kind in kinds:
            for way in (0, 1):
                relay(kind, way, s)

    for n, tab in enumerate((sk, sv)):
        wait_bytes(tab.at[:, z], kv_recv.at[n])
        for way in (0, 1):
            if steps(n, way) > 0:
                ring_copy(n, way, 0, piece(n, z), z).start()
    ring_step(1, (2, 3))
    ring_step(1, (0, 1))
    send_queries()
    acc[...] = jnp.zeros_like(acc)
    peak[...] = jnp.full(peak.shape, -1e30, jnp.float32)

    def queries_of(yp, group):
        parts = [
            qb[pl.ds(yp * nh, nh), :, head_cols(group * GROUP + j, HD)].reshape(BLK, HD)
            for j in range(GROUP)
        ]
        return jnp.concatenate(parts, axis=0)

    def fold(yp, group, keys, values, mask, keep):
        s = lax.dot_general(queries_of(yp, group), keys, NT, preferred_element_type=jnp.float32)
        if mask is not None:
            n = s.shape[1] - mask.shape[1]
            tail = s[:, n:] + jnp.concatenate([mask] * GROUP, axis=0)
            s = jnp.concatenate([s[:, :n], tail], axis=1) if n else tail
        values = jnp.concatenate([values, jnp.ones_like(values)], axis=1)
        heads = pl.ds(yp * QPG + group * GROUP, GROUP)
        m1 = peak[heads].reshape(GROUP * BLK, HD)
        m = jnp.maximum(m1, jnp.max(s, axis=1, keepdims=True) * SCALE)
        mm = jnp.concatenate([m] * (s.shape[1] // HD), axis=1)
        w = jnp.exp2(s * SCALE - mm).astype(jnp.bfloat16)
        r = lax.dot_general(w, values, NN, preferred_element_type=jnp.float32)
        fade = jnp.exp2(m1 - m)
        fade = jnp.concatenate([fade, fade], axis=1)
        a = acc[heads].reshape(GROUP * BLK, 2 * HD) * fade + r
        if keep:
            acc[heads] = a.reshape(GROUP, BLK, 2 * HD)
            peak[heads] = m.reshape(GROUP, BLK, HD)
        return m, a

    def take_chunk(chunk):
        places = [
            lax.rem(z + 2 * chunk, nz),
            lax.rem(z + nz - 2 * chunk - 1, nz),
            lax.rem(z + 2 * chunk + 1, nz),
            lax.rem(z + nz - 2 * chunk - 2, nz),
        ]
        row = lax.broadcasted_iota(jnp.int32, (BLK, 4 * stripe), 0)
        col = lax.broadcasted_iota(jnp.int32, (BLK, 4 * stripe), 1)
        key_pos = lax.rem(col, stripe) + y * stripe
        for i, place in enumerate(places):
            key_pos = key_pos + jnp.where(lax.div(col, stripe) == i, place * BLK, 0)
            for yp in range(ny):
                rows_i = slice(i * stripe, (i + 1) * stripe)
                kc[yp, rows_i, :] = sk[yp, place]
                vc[yp, rows_i, :] = sv[yp, place]
        bias[...] = jnp.where(key_pos <= z * BLK + row, 0.0, -1e30).astype(jnp.float32)

    def span_part(t, blocks):
        for yp in blocks:
            n = (yp + 1) * 4 * stripe
            keys = kc[0 : yp + 1].reshape(n, HD)
            values = vc[0 : yp + 1].reshape(n, HD)
            fold(yp, t, keys, values, bias[...], True)

    chunks = half // 2 - 1
    first = half - chunks

    def step_body(s, _):
        late = s >= first
        ring_step(s, (2,))
        pl.when(s == first)(functools.partial(wait_bytes, qb, q_recv))
        pl.when(late)(lambda: take_chunk(s - first))
        pl.when(late)(lambda: span_part(0, range(ny - 1, ny)))
        ring_step(s, (0,))
        pl.when(late)(lambda: span_part(0, range(ny - 1)))
        ring_step(s, (3,))
        pl.when(late)(lambda: span_part(1, range(ny - 1, ny)))
        ring_step(s, (1,))
        pl.when(late)(lambda: span_part(1, range(ny - 1)))
        return 0

    lax.fori_loop(2, half, step_body, 0)
    ring_step(half, (2, 3))
    if chunks == 0:
        wait_bytes(qb, q_recv)
    own_k.wait()
    own_v.wait()
    for copy in indices:
        copy.wait()

    def prefix(yp):
        for i in range(SEL):
            block = lists_s[i, yp * nz + z]
            at = hold[block] * HOLD_BLK + slot[block]
            kp[i * stripe : (i + 1) * stripe, :] = pk[at]
            vp[i * stripe : (i + 1) * stripe, :] = pv[at]
        for group in range(QPG // GROUP):
            fold(yp, group, kp[...], vp[...], None, True)

    lane = lax.broadcasted_iota(jnp.int32, (BLK, HD), 1)
    order = sorted(range(ny), key=lambda o: (o == 0, -min(o, ny - o)))
    for o in order:
        yp = ys[o]
        prefix(yp)
        if o == order[0]:
            ring_step(half, (0, 1))
            take_chunk(half // 2 - 1)
        keys = kc[...].reshape(ny * 4 * stripe, HD)
        values = vc[...].reshape(ny * 4 * stripe, HD)
        mask = jnp.concatenate(
            [
                jnp.where(jnp.full(bias.shape, i, jnp.int32) < yp, 0.0, bias[...])
                + jnp.where(jnp.full(bias.shape, i, jnp.int32) > yp, -1e30, 0.0)
                for i in range(ny)
            ],
            axis=1,
        )
        for group in range(QPG // GROUP):
            m, a = fold(yp, group, keys, values, mask, False)
            total = a[:, HD:]
            mixed = (a[:, :HD] / total).astype(jnp.bfloat16)
            lse = m + jnp.log2(total)
            level = jnp.zeros((BLK, HD), jnp.float32)
            for j in range(GROUP):
                rows_j = slice(j * BLK, (j + 1) * BLK)
                cols = slice((group * GROUP + j) * HD, (group * GROUP + j + 1) * HD)
                sendo[yp, :, cols] = mixed[rows_j]
                level = jnp.where(lane == j, lse[rows_j], level)
            sendl[yp, group] = level.T[:8]
            if o:
                cols = slice(group * GROUP * HD, (group + 1) * GROUP * HD)
                for n, (src, dst) in enumerate(
                    (
                        (sendl.at[yp, group], recvl.at[y, group]),
                        (sendo.at[yp, :, cols], recvo.at[y, :, cols]),
                    )
                ):
                    pltpu.make_async_remote_copy(
                        src_ref=src,
                        dst_ref=dst,
                        send_sem=o_send.at[n, o, group],
                        recv_sem=o_recv.at[n, o, group],
                        device_id={"segment": yp},
                    ).start()

    fill = jnp.zeros((BLK - 8, BLK), jnp.float32)
    for group in range(QPG // GROUP):
        cols = slice(group * GROUP * HD, (group + 1) * GROUP * HD)
        levels = [sendl[y, group]]
        parts = [sendo.at[y]]
        for o in order[:-1]:
            src = lax.rem(y + ny - o, ny)
            wait_bytes(recvl.at[src, group], o_recv.at[0, o, group])
            wait_bytes(recvo.at[src, :, cols], o_recv.at[1, o, group])
            levels.append(recvl[src, group])
            parts.append(recvo.at[src])
        top = functools.reduce(jnp.maximum, levels)
        shares = [jnp.exp2(v - top) for v in levels]
        norm = 1.0 / functools.reduce(jnp.add, shares)
        shares = [jnp.concatenate([v * norm, fill], axis=0).T for v in shares]
        for j in range(GROUP):
            cols = slice((group * GROUP + j) * HD, (group * GROUP + j + 1) * HD)
            out[:, cols] = functools.reduce(
                jnp.add,
                [
                    w[:, j : j + 1] * part[:, cols].astype(jnp.float32)
                    for w, part in zip(shares, parts)
                ],
            ).astype(jnp.bfloat16)

    wait_bytes(qb.at[: plane - 1], q_send)
    for n, src in enumerate((k_in, v_in)):
        pl.when(target == y)(
            functools.partial(wait_bytes, src.at[:, : (nh - 1) * HD], kv_send.at[n])
        )
        pl.when(target != y)(functools.partial(wait_bytes, src, kv_send.at[n]))
    for kind in range(4):
        for way in (0, 1):
            count = steps(kind, way)

            def sent(step, _, kind=kind, way=way):
                wait_bytes(piece(kind, z), ring_send.at[kind * 2 + way, step])
                return 0

            lax.fori_loop(0, count, sent, 0)
    for o in range(1, ny):
        for group in range(QPG // GROUP):
            wait_bytes(sendl.at[0, group], o_send.at[0, o, group])
            wait_bytes(sendo.at[0, :, : GROUP * HD], o_send.at[1, o, group])


def local(ny, nz, nh, q, k, v, ck, cv, hold, slot, lists):
    rows, width, stripe = BLK // nh, QPG * HD, BLK // ny
    blocks = ck.shape[0] * nz
    ck = ck.reshape(ck.shape[0], BLK, HD)
    cv = cv.reshape(cv.shape[0], BLK, HD)
    lists = jnp.transpose(lists, (1, 2, 0))
    hbm = pl.BlockSpec(memory_space=pltpu.HBM)
    bf, f32, dma = jnp.bfloat16, jnp.float32, pltpu.SemaphoreType.DMA
    return pl.pallas_call(
        functools.partial(kernel, ny, nz, nh),
        out_shape=jax.ShapeDtypeStruct((BLK, width), bf),
        in_specs=[hbm] * 8,
        out_specs=pl.BlockSpec(memory_space=pltpu.VMEM),
        scratch_shapes=[
            pltpu.VMEM((ny * nh, rows, width), bf),
            pltpu.VMEM((ny, nz, stripe, HD), bf),
            pltpu.VMEM((ny, nz, stripe, HD), bf),
            pltpu.VMEM((blocks, stripe, HD), bf),
            pltpu.VMEM((blocks, stripe, HD), bf),
            pltpu.VMEM((ny, 4 * stripe, HD), bf),
            pltpu.VMEM((ny, 4 * stripe, HD), bf),
            pltpu.VMEM((BLK, 4 * stripe), f32),
            pltpu.VMEM((ny * QPG, BLK, 2 * HD), f32),
            pltpu.VMEM((ny * QPG, BLK, HD), f32),
            pltpu.VMEM((ny, BLK, width), bf),
            pltpu.VMEM((ny, BLK, width), bf),
            pltpu.VMEM((ny, QPG // GROUP, 8, BLK), f32),
            pltpu.VMEM((ny, QPG // GROUP, 8, BLK), f32),
            pltpu.VMEM((SEL * stripe, HD), bf),
            pltpu.VMEM((SEL * stripe, HD), bf),
            pltpu.SMEM((SEL, lists.shape[2]), jnp.int32),
            pltpu.SMEM(hold.shape, jnp.int32),
            pltpu.SMEM(slot.shape, jnp.int32),
            dma, dma, dma((2,)), dma((2,)),
            dma((8, nz // 2)), dma((8, nz // 2)),
            dma((2, ny, QPG // GROUP)), dma((2, ny, QPG // GROUP)),
            dma((2,)), dma((3,)),
        ],
        compiler_params=pltpu.CompilerParams(
            collective_id=0, has_side_effects=True, vmem_limit_bytes=60 * 2**20
        ),
        cost_estimate=pl.CostEstimate(
            flops=4 * BLK * QPG * HD * 6144, bytes_accessed=2**24, transcendentals=6144 * 1024
        ),
        name="attend",
    )(q, k, v, ck, cv, hold, slot, lists)


def solution(mesh):
    ny, nz, nh = mesh.shape["segment"], mesh.shape["seq"], mesh.shape["head"]
    placed = (
        P(("segment", "seq", "head"), None),
        P(("segment", "seq", "head"), None),
        P(("segment", "seq", "head"), None),
        P("seq", None, "head", None),
        P("seq", None, "head", None),
        P(),
        P(),
        P(),
    )
    return jax.shard_map(
        functools.partial(local, ny, nz, nh),
        mesh=mesh,
        in_specs=placed,
        out_specs=P(("segment", "seq"), "head"),
        check_vma=False,
    )
```
